32 devices in a mesh: groups: 2 (over x), req: 2 (over core), tensor: 8 (over z, y).
Axes of the slice: x: 2, y: 2, z: 4, core: 2. Of those that a mesh axis runs over, the one named last changes fastest.
Arguments:
- hidden: bfloat16 [4096, 28672], P(('groups', 'req'), 'tensor'), parts along dimension 0, may hold values from -6 to 6
- down_matrix: bfloat16 [28672, 8192], P('tensor'), may hold values from -0.046875 to 0.046875
- shrink_factors: bfloat16 [64, 64, 28672], P('req', None, 'tensor'), may hold values from -0.03125 to 0.03125
- expand_factors: bfloat16 [64, 64, 8192], P('req', None, 'tensor'), may hold values from -0.75 to 0.75
- request_adapter: int32 [4, 8], P(('groups', 'req')), parts along dimension 0, may hold values from 0 to 63
- request_lengths: int32 [4, 8], P(('groups', 'req')), parts along dimension 0, may hold values from 1 to 512, 1024 in all within a row
- adapter_rank_table: int32 [64], replicated, may hold values from 16 to 64, as said below
- adapter_stored_row: int32 [64], replicated, may hold values from 0 to 63, each once
Outputs:
- layer_out: bfloat16 [4096, 8192], P(('groups', 'req'), 'tensor'), parts along dimension 0
The draws below stay inside these ranges and needn't reach their ends.
There are 2 independent parts, one for each index of `groups`. The reference program is written for one: setup_inputs(seed, part) draws one part's arguments, and reference() takes and returns one part's arrays. A program takes and returns all parts, laid end to end along the dimension named above; an argument that names none is the same for every part. Nothing has to cross between parts.
Inputs may be any that keep to these rules, and one draw needn't show every extreme that they name: `adapter_rank_table`: every rank from 16 to 64 may occur; both ends occur in every draw. `request_lengths`: each row sums to 1024; its largest entry is exactly 512. `adapter_stored_row`: each stored row holds exactly one adapter.
All inputs are finite; a program needn't handle non-finite values.
Results may differ from the reference program's by a relative error of at most 0.004.
Values may be sent and summed in bfloat16 or wider, within the bound.
A program may use at most 256 MiB of HBM per device.

```python
import math
import jax
import jax.numpy as jnp
import numpy as np
from jax import lax

MODEL_WIDTH = 8192
HIDDEN_WIDTH = 28672
RANK_LIMIT = 64
RMIN = 16
TOK_DEV = 1024
REQ_DEV = 8
LEN_MOST = 512
TOKENS = 2048
ADAPTER_COUNT = 64
N_REQ = 2


def draw_adapter_rank_table(key, part):
    key = jax.random.fold_in(key, 7)
    first_key, second_key, third_key = jax.random.split(key, 3)
    ranks = jax.random.randint(first_key, (ADAPTER_COUNT,), RMIN, RANK_LIMIT + 1)
    high_spot = jax.random.randint(second_key, (), 0, ADAPTER_COUNT)
    low_spot = (high_spot + 1 + jax.random.randint(third_key, (), 0, ADAPTER_COUNT - 1)) % ADAPTER_COUNT
    places = jnp.arange(ADAPTER_COUNT)
    ranks = jnp.where(places == high_spot, RANK_LIMIT, ranks)
    ranks = jnp.where(places == low_spot, RMIN, ranks)
    return ranks.astype(jnp.int32)


def set_ends(values, own_key, smallest, high):
    shape = values.shape
    place = [jax.random.randint(jax.random.fold_in(own_key, axis), (), 0, shape[axis]) for axis in range(len(shape))]
    values = values.at[tuple(place)].set(smallest)
    longest = shape.index(max(shape))
    place[longest] = (place[longest] + 1) % shape[longest]
    return values.at[tuple(place)].set(high)


def spiked(drawn, stream_key, source, target, parts, factor):
    owner, partner = [(jnp.arange(drawn.shape[dim]) // (drawn.shape[dim] // parts)).reshape([-1 if axis == dim else 1 for axis in range(drawn.ndim)]) for dim in (source, target)]
    chosen = jax.random.permutation(stream_key, parts)[partner]
    strong = (owner == chosen) | (owner == (partner + parts // 2) % parts)
    return jnp.where(strong, factor * drawn, drawn)


def steps_of(rng, extent, pieces, smallest, largest):
    loudness = 1.0
    for position, blocks in pieces:
        steps = jax.random.uniform(jax.random.fold_in(jax.random.fold_in(rng, 6), position), (blocks,), jnp.float32, smallest / len(pieces), largest / len(pieces))
        loudness = loudness * jnp.repeat(jnp.exp(steps), extent[position] // blocks).reshape((-1,) + (1,) * (len(extent) - 1 - position))
    return loudness


def rank_bounds(number_of, skew):
    weights = [(1 << 20) // math.isqrt(grade ** skew) + 1 for grade in range(1, number_of + 1)]
    deviation = 1 + sum(weights) // (1 << 30)
    return np.cumsum(np.array([max(1, weight // deviation) for weight in weights]))


def ranked(own_key, dims, number_of, slope):
    listing = rank_bounds(number_of, slope)
    pick = jax.random.randint(jax.random.fold_in(own_key, 1), dims, 0, int(listing[number_of - 1]))
    rank = jnp.searchsorted(jnp.asarray(listing, jnp.int32), pick, side="right")
    return jax.random.permutation(jax.random.fold_in(own_key, 2), number_of)[rank].astype(jnp.int32)


def profile(number_of, total, limit, skew):
    weights = [(1 << 20) // math.isqrt(grade ** skew) + 1 for grade in range(2, number_of + 1)]
    rest, counts = total - limit - (number_of - 1), [1] * (number_of - 1)
    while rest > 0:
        free = [i for i in range(number_of - 1) if counts[i] < limit]
        pool, budget = sum([weights[i] for i in free]), rest
        for i in free:
            addition = min(limit - counts[i], max(1, budget * weights[i] // pool), rest)
            counts[i] = counts[i] + addition
            rest = rest - addition
    return np.array([limit] + counts)


def ragged_sizes(stream_key, number_of, total, bound, slope):
    if number_of == 2:
        one = jax.random.randint(stream_key, (), max(1, total - bound), min(bound, total - 1) + 1)
        return jnp.stack([one, total - one])
    sizes = jnp.asarray(profile(number_of, total, bound, slope), jnp.int32)
    couples = (number_of - 1) // 2
    giver, sink = sizes[1:1 + 2 * couples:2], sizes[2:2 + 2 * couples:2]
    margin = jnp.minimum(giver - 1, bound - sink)
    moved = jax.random.randint(jax.random.fold_in(stream_key, 1), (couples,), 0, 1 << 20) % (margin + 1)
    sizes = sizes.at[1:1 + 2 * couples:2].set(giver - moved).at[2:2 + 2 * couples:2].set(sink + moved)
    return sizes[jax.random.permutation(jax.random.fold_in(stream_key, 2), number_of)]


def bell_draw(own_key, dims, spread, most, cuts=(), kind=jnp.bfloat16):
    array = spread * jax.random.normal(own_key, dims, jnp.float32)
    if cuts:
        array = array * steps_of(own_key, dims, cuts, -0.22, 0.18)
    return jnp.clip(array, -most, most).astype(kind)


def gaussian_with(key, dims, deviation, most, cuts, heavy, kind=jnp.bfloat16):
    values = deviation * jax.random.normal(key, dims, jnp.float32)
    if cuts:
        values = values * steps_of(key, dims, cuts, -0.22, 0.18)
    return jnp.clip(spiked(values, jax.random.fold_in(key, 3), *heavy), -most, most).astype(kind)


def setup_inputs(seed: int = 0, part: int = 0) -> dict:
    splits = jax.random.split(jax.random.key(seed), 9)
    part_keys = jax.random.split(jax.random.fold_in(splits[8], part), 9)
    hidden = bell_draw(part_keys[0], (TOKENS, HIDDEN_WIDTH), 1.0, 6.0, ((0, 2), (1, 8)))
    down_matrix = gaussian_with(splits[1], (HIDDEN_WIDTH, MODEL_WIDTH), HIDDEN_WIDTH ** -0.5, 0.046875, ((0, 8),), (0, 1, 8, 2.0))
    shrink_factors = bell_draw(splits[2], (ADAPTER_COUNT, RANK_LIMIT, HIDDEN_WIDTH), HIDDEN_WIDTH ** -0.5, 0.03125, ((0, 2), (2, 8)))
    expand_factors = bell_draw(splits[3], (ADAPTER_COUNT, RANK_LIMIT, MODEL_WIDTH), RANK_LIMIT ** -0.5, 0.75, ((0, 2), (2, 8)))
    request_adapter = set_ends(ranked(part_keys[4], (N_REQ, REQ_DEV), ADAPTER_COUNT, 2), jax.random.fold_in(part_keys[4], 3), 0, ADAPTER_COUNT - 1).astype(jnp.int32)
    request_lengths = jax.vmap(lambda own: ragged_sizes(own, REQ_DEV, TOK_DEV, LEN_MOST, 1))(jax.random.split(part_keys[5], N_REQ)).reshape((N_REQ, REQ_DEV)).astype(jnp.int32)
    adapter_rank_table = draw_adapter_rank_table(jax.random.fold_in(splits[8], 71), part)
    adapter_stored_row = jax.random.permutation(splits[7], ADAPTER_COUNT).astype(jnp.int32)
    return {"hidden": hidden, "down_matrix": down_matrix, "shrink_factors": shrink_factors, "expand_factors": expand_factors, "request_adapter": request_adapter, "request_lengths": request_lengths, "adapter_rank_table": adapter_rank_table, "adapter_stored_row": adapter_stored_row}


adapter_scale_factor = 16.0


def reference(hidden, down_matrix, shrink_factors, expand_factors, request_adapter, request_lengths, adapter_rank_table, adapter_stored_row):
    seg_ends = jnp.cumsum(request_lengths, axis=1).astype(jnp.int32)
    positions = jnp.arange(TOK_DEV, dtype=jnp.int32)
    local_req = jnp.sum((positions[None, :, None] >= seg_ends[:, None, :]).astype(jnp.int32), axis=2)
    shard_base = REQ_DEV * jnp.arange(N_REQ, dtype=jnp.int32)
    req_of_tok = (local_req + shard_base[:, None]).reshape(-1).astype(jnp.int32)
    flat_ids = request_adapter.reshape(-1).astype(jnp.int32)
    req_rank = adapter_rank_table[flat_ids]
    request_stored_row = adapter_stored_row[flat_ids]
    onehot = req_of_tok[:, None] == jnp.arange(N_REQ * REQ_DEV, dtype=jnp.int32)[None, :]
    adapter_shrink_rows = shrink_factors[request_stored_row].astype(jnp.float32)
    shrink_all = jnp.einsum("tf,jrf->tjr", hidden.astype(jnp.float32), adapter_shrink_rows, precision=lax.Precision.HIGHEST)
    live = jnp.arange(RANK_LIMIT, dtype=jnp.int32)[None, None, :] < req_rank[None, :, None]
    shrink_result = jnp.sum(jnp.where(onehot[:, :, None] & live, shrink_all, jnp.float32(0.0)), axis=1)
    token_rank = jnp.sum(jnp.where(onehot, req_rank[None, :], 0), axis=1)
    scaled_result = (shrink_result * (adapter_scale_factor / token_rank.astype(jnp.float32))[:, None]).astype(jnp.bfloat16)
    widened_shrink = jnp.where(onehot[:, :, None], scaled_result.astype(jnp.float32)[:, None, :], jnp.float32(0.0))
    adapter_expand_rows = expand_factors[request_stored_row].astype(jnp.float32)
    adapter_output = jnp.einsum("woa,oav->wv", widened_shrink, adapter_expand_rows, precision=lax.Precision.HIGHEST)
    base_output = jnp.dot(hidden, down_matrix, preferred_element_type=jnp.float32)
    return (base_output + adapter_output).astype(jnp.bfloat16)
```

```python
import jax
import jax.numpy as jnp
from jax import lax
from jax.sharding import PartitionSpec as P

adapter_scale_factor = 16.0
ZFIRST = 0


def lookup(values_table, id_list):
    matches = id_list[:, None] == jnp.arange(values_table.shape[0], dtype=jnp.int32)[None, :]
    return jnp.sum(jnp.where(matches, values_table[None, :], 0), axis=1)


def token_layout(request_lengths, req_count, tok_count):
    seg_ends = jnp.cumsum(request_lengths[0])
    positions = jnp.arange(tok_count, dtype=jnp.int32)
    req_of_tok = jnp.sum((positions[:, None] >= seg_ends[None, :]).astype(jnp.int32), axis=1)
    return req_of_tok[:, None] == jnp.arange(req_count, dtype=jnp.int32)[None, :]


def factor(count):
    inner = 1
    while inner * inner * 4 <= count:
        inner *= 2
    return count // inner, inner


def line_reduce(own, size, place, hop):
    total = own(place)
    if size == 1:
        return total
    if size == 2:
        return total + hop(own(1 - place).astype(jnp.bfloat16), [(0, 1), (1, 0)]).astype(jnp.float32)
    for sign in (1, -1):
        got = None
        for step in range(size - 1):
            if sign == 1:
                dest = size - 1 - step + place
                pairs = [(z, z + 1) for z in range(step + 1)]
            else:
                dest = step - size + 1 + place
                pairs = [(z, z - 1) for z in range(size - 1 - step, size)]
            block = own(jnp.clip(dest, 0, size - 1))
            if got is not None:
                block = block + got.astype(jnp.float32)
            got = hop(block.astype(jnp.bfloat16), pairs)
        total = total + got.astype(jnp.float32)
    return total


def fetch_rows(pool, my_slots, other_slots, half, size):
    per = pool.shape[0]
    low = half * per

    def local(slots):
        return pool[jnp.clip(slots - low, 0, per - 1)]

    rows = local(my_slots)
    got_rows = []
    for shift in range(1, size):
        pairs = [(r, (r - shift) % size) for r in range(size)]
        got_rows.append(lax.ppermute(local(other_slots[shift - 1]), "req", pairs))
    for shift in range(1, size):
        theirs = my_slots // per == (half + shift) % size
        rows = jnp.where(theirs[:, None, None], got_rows[shift - 1], rows)
    return rows


def make_per_device(n_tensor, n_req):
    n_outer, n_inner = factor(n_tensor)

    def hop_outer(block, pairs):
        full = [(a * n_inner + i, b * n_inner + i) for a, b in pairs for i in range(n_inner)]
        return lax.ppermute(block, "tensor", full)

    def hop_inner(block, pairs):
        full = [(o * n_inner + a, o * n_inner + b) for a, b in pairs for o in range(n_outer)]
        return lax.ppermute(block, "tensor", full)

    def per_device(
        hidden,
        down_matrix,
        shrink_factors,
        expand_factors,
        request_adapter,
        request_lengths,
        adapter_rank_table,
        adapter_stored_row,
    ):
        tok_count = hidden.shape[0]
        req_count = request_adapter.shape[1]
        largest_rank = shrink_factors.shape[1]
        local_width = expand_factors.shape[2]
        me = lax.axis_index("tensor")
        half = lax.axis_index("req")
        outer, inner = me // n_inner, me % n_inner

        chunks = max(1, min(4, local_width // 128))
        sub = local_width // chunks

        def partial(dest_outer, dest_inner, chunk):
            start = (dest_outer * n_inner + dest_inner) * local_width + chunk * sub
            weights = lax.dynamic_slice_in_dim(down_matrix, start, sub, axis=1)
            return jnp.dot(hidden, weights, preferred_element_type=jnp.float32)

        def pick(stack):
            return lambda index: lax.dynamic_index_in_dim(stack, index, 0, keepdims=False)

        def reduce_chunk(chunk):
            def column(dest_inner):
                return jnp.stack([partial(o, dest_inner, chunk) for o in range(n_outer)])

            if n_inner <= 2:
                own = column
            else:
                own = pick(jnp.stack([column(i) for i in range(n_inner)]))
            folded = line_reduce(own, n_inner, inner, hop_inner)
            return line_reduce(pick(folded), n_outer, outer, hop_outer)

        pieces = [reduce_chunk(chunk) for chunk in range(chunks)]

        all_ids = lax.all_gather(request_adapter[0], "req", axis=0)
        my_ids = request_adapter[0]
        my_ranks = lookup(adapter_rank_table, my_ids)
        my_slots = lookup(adapter_stored_row, my_ids)
        other_slots = [
            lookup(adapter_stored_row, all_ids[(half - shift) % n_req]) for shift in range(1, n_req)
        ]
        adapter_shrink_rows = fetch_rows(shrink_factors, my_slots, other_slots, half, n_req)
        adapter_expand_rows = fetch_rows(expand_factors, my_slots, other_slots, half, n_req)
        onehot = token_layout(request_lengths, req_count, tok_count)
        flat_a = adapter_shrink_rows.reshape(req_count * largest_rank, adapter_shrink_rows.shape[2])
        shrink_all = lax.dot_general(
            hidden, flat_a, (((1,), (1,)), ((), ())), preferred_element_type=jnp.float32
        )
        shrink_all = shrink_all.reshape(tok_count, req_count, largest_rank)
        live = jnp.arange(largest_rank, dtype=jnp.int32)[None, None, :] < my_ranks[None, :, None]
        keep_mask = onehot[:, :, None] & live
        shrink_result = jnp.sum(jnp.where(keep_mask, shrink_all, 0.0), axis=1)
        token_rank = jnp.sum(jnp.where(onehot, my_ranks[None, :], 0), axis=1)
        token_scale = adapter_scale_factor / token_rank.astype(jnp.float32)
        folded = lax.psum(shrink_result.reshape(tok_count // 2, 2 * largest_rank), "tensor")
        scaled_result = (folded.reshape(tok_count, largest_rank) * token_scale[:, None]).astype(
            jnp.bfloat16
        )
        token_spread = jnp.where(
            onehot[:, :, None], scaled_result[:, None, :], jnp.zeros((), jnp.bfloat16)
        )
        token_spread = token_spread.reshape(tok_count, req_count * largest_rank)
        flattened_expand = adapter_expand_rows.reshape(req_count * largest_rank, local_width)
        adapter_piece = jnp.dot(token_spread, flattened_expand, preferred_element_type=jnp.float32)
        return (jnp.concatenate(pieces, axis=1) + adapter_piece).astype(jnp.bfloat16)

    return per_device


def solution(mesh):
    in_specs = (
        P(("groups", "req"), "tensor"),
        P("tensor", None),
        P("req", None, "tensor"),
        P("req", None, "tensor"),
        P(("groups", "req"), None),
        P(("groups", "req"), None),
        P(),
        P(),
    )
    out_specs = P(("groups", "req"), "tensor")
    per_device = make_per_device(mesh.shape["tensor"], mesh.shape["req"])
    return jax.shard_map(
        per_device, mesh=mesh, in_specs=in_specs, out_specs=out_specs, check_vma=False
    )
```

```python
import functools

import jax
import jax.numpy as jnp
from jax import lax
from jax.experimental import pallas as pl
from jax.experimental.pallas import tpu as pltpu
from jax.sharding import PartitionSpec as P

adapter_scale_factor = 16.0
ROWS = 256
MESH = pl.DeviceIdType.MESH
ZFIRST = 0


def lookup(values_table, id_list):
    matches = id_list[:, None] == jnp.arange(values_table.shape[0], dtype=jnp.int32)[None, :]
    return jnp.sum(jnp.where(matches, values_table[None, :], 0), axis=1)


def token_layout(request_lengths, req_count, tok_count):
    seg_ends = jnp.cumsum(request_lengths[0])
    positions = jnp.arange(tok_count, dtype=jnp.int32)
    req_of_tok = jnp.sum((positions[:, None] >= seg_ends[None, :]).astype(jnp.int32), axis=1)
    return req_of_tok[:, None] == jnp.arange(req_count, dtype=jnp.int32)[None, :]


def reduce_kernel(
    n_outer,
    rows,
    sub,
    hidden_hbm,
    down_hbm,
    out_hbm,
    hidden,
    tiles,
    y_send,
    y_got,
    own,
    z_got,
    load_sem,
    tile_sems,
    y_send_sem,
    y_got_sems,
    z_send_sem,
    z_got_sems,
    out_sem,
):
    tok_count = hidden.shape[0]
    pieces = tok_count // rows
    rounds = y_send.shape[0]
    chunks = rounds // pieces
    width = chunks * sub
    me = lax.axis_index("tensor")
    z, y = me // 2, me % 2
    last = n_outer - 1

    def device(index):
        return {"tensor": index}

    pair = z * 2 + (1 - y)
    above = (z + 1) * 2 + y
    below = (z - 1) * 2 + y

    def weights(dest_z, dest_y, chunk, slot):
        start = pl.multiple_of((dest_z * 2 + dest_y) * width + chunk * sub, 128)
        return pltpu.make_async_copy(
            down_hbm.at[:, pl.ds(start, sub)], tiles.at[slot], tile_sems.at[slot]
        )

    load = pltpu.make_async_copy(hidden_hbm, hidden, load_sem)
    load.start()
    weights(0, 1 - y, 0, 0).start()

    barrier = pltpu.get_barrier_semaphore()
    pl.semaphore_signal(barrier, inc=1, device_id=device(pair), device_id_type=MESH)

    @pl.when(z < last)
    def _():
        pl.semaphore_signal(barrier, inc=1, device_id=device(above), device_id_type=MESH)

    @pl.when(z > 0)
    def _():
        pl.semaphore_signal(barrier, inc=1, device_id=device(below), device_id_type=MESH)

    pl.semaphore_wait(barrier, 1 + jnp.minimum(z, 1) + jnp.minimum(last - z, 1))

    load.wait()

    def y_copy(rnd, dest):
        return pltpu.make_async_remote_copy(
            src_ref=y_send.at[rnd, dest],
            dst_ref=y_got.at[rnd, dest],
            send_sem=y_send_sem,
            recv_sem=y_got_sems.at[rnd, dest],
            device_id=device(pair),
            device_id_type=MESH,
        )

    def z_copy(rnd, dest, slot, target):
        return pltpu.make_async_remote_copy(
            src_ref=y_got.at[rnd, dest],
            dst_ref=z_got.at[rnd, slot],
            send_sem=z_send_sem,
            recv_sem=z_got_sems.at[rnd, slot],
            device_id=device(target),
            device_id_type=MESH,
        )

    def product(slot, piece):
        return jnp.dot(
            hidden[pl.ds(pl.multiple_of(piece * rows, rows), rows), :],
            tiles[slot],
            preferred_element_type=jnp.float32,
        )

    total_tiles = chunks * n_outer

    @pl.loop(0, total_tiles)
    def _(index):
        chunk, dest = index // n_outer, index % n_outer
        slot = index % 2

        @pl.when(index + 1 < total_tiles)
        def _():
            weights((index + 1) % n_outer, 1 - y, (index + 1) // n_outer, (index + 1) % 2).start()

        @pl.when(index + 1 == total_tiles)
        def _():
            weights(0, y, 0, total_tiles % 2).start()

        weights(dest, 1 - y, chunk, slot).wait()

        @pl.loop(0, pieces)
        def _(piece):
            rnd = chunk * pieces + piece
            y_send[rnd, dest] = product(slot, piece).astype(jnp.bfloat16)

            @pl.when(chunk == 0)
            def _():
                y_copy(rnd, dest).start()

        @pl.when((chunk > 0) & (dest == last))
        def _():
            @pl.loop(0, pieces * n_outer)
            def _(item):
                y_copy(chunk * pieces + item // n_outer, item % n_outer).start()

    def own_tiles(chunk):
        @pl.loop(0, n_outer)
        def _(dest):
            index = chunk * n_outer + dest
            slot = (total_tiles + index) % 2

            @pl.when(index + 1 < total_tiles)
            def _():
                weights(
                    (index + 1) % n_outer, y, (index + 1) // n_outer, (total_tiles + index + 1) % 2
                ).start()

            weights(dest, y, chunk, slot).wait()

            @pl.loop(0, pieces)
            def _(piece):
                own[chunk * pieces + piece, dest] = product(slot, piece)

    def out_copy(rnd):
        chunk, piece = rnd // pieces, rnd % pieces
        return pltpu.make_async_copy(
            own.at[rnd, z],
            out_hbm.at[
                pl.ds(pl.multiple_of(piece * rows, rows), rows),
                pl.ds(pl.multiple_of(chunk * sub, 128), sub),
            ],
            out_sem,
        )

    @pl.loop(0, rounds + last)
    def _(step):
        @pl.when((step < rounds) & (step % pieces == 0))
        def _():
            own_tiles(step // pieces)

        @pl.loop(0, n_outer)
        def _(dest):
            def pair_sum(rnd):
                y_copy(rnd, dest).wait_recv()
                own[rnd, dest] = own[rnd, dest] + y_got[rnd, dest].astype(jnp.float32)

            def add_line(rnd, slot):
                z_copy(rnd, dest, slot, pair).wait_recv()
                own[rnd, dest] = own[rnd, dest] + z_got[rnd, slot].astype(jnp.float32)

            up_round = step - z

            @pl.when((dest > z) & (up_round >= 0) & (up_round < rounds))
            def _():
                pair_sum(up_round)

                @pl.when(z > 0)
                def _():
                    add_line(up_round, dest)

                y_got[up_round, dest] = own[up_round, dest].astype(jnp.bfloat16)
                z_copy(up_round, dest, dest, above).start()

            down_round = step - (last - z)

            @pl.when((dest < z) & (down_round >= 0) & (down_round < rounds))
            def _():
                pair_sum(down_round)

                @pl.when(z < last)
                def _():
                    add_line(down_round, dest)

                y_got[down_round, dest] = own[down_round, dest].astype(jnp.bfloat16)
                slot = jnp.where(dest == z - 1, n_outer, dest)
                z_copy(down_round, dest, slot, below).start()

            end_round = step - jnp.maximum(z, last - z)

            @pl.when((dest == z) & (end_round >= 0) & (end_round < rounds))
            def _():
                pair_sum(end_round)

                @pl.when(z > 0)
                def _():
                    add_line(end_round, dest)

                @pl.when(z < last)
                def _():
                    add_line(end_round, n_outer)

                out_copy(end_round).start()

    pltpu.make_async_copy(y_send, y_got, y_send_sem).wait()

    if last > 0:
        moved = z_got.at[:, pl.ds(0, last)]
        pltpu.make_async_copy(moved, moved, z_send_sem).wait()

    pltpu.make_async_copy(out_hbm, out_hbm, out_sem).wait()


def reduced_product(hidden, down_matrix, n_tensor):
    tok_count, depth = hidden.shape
    total_width = down_matrix.shape[1]
    width = total_width // n_tensor
    n_outer = n_tensor // 2
    sub = min(256, width)
    rows = min(ROWS, tok_count)
    rounds = (width // sub) * (tok_count // rows)
    return pl.pallas_call(
        functools.partial(reduce_kernel, n_outer, rows, sub),
        out_shape=jax.ShapeDtypeStruct((tok_count, width), jnp.float32),
        in_specs=[pl.BlockSpec(memory_space=pl.ANY)] * 2,
        out_specs=pl.BlockSpec(memory_space=pl.ANY),
        scratch_shapes=[
            pltpu.VMEM((tok_count, depth), jnp.bfloat16),
            pltpu.VMEM((2, depth, sub), jnp.bfloat16),
            pltpu.VMEM((rounds, n_outer, rows, sub), jnp.bfloat16),
            pltpu.VMEM((rounds, n_outer, rows, sub), jnp.bfloat16),
            pltpu.VMEM((rounds, n_outer, rows, sub), jnp.float32),
            pltpu.VMEM((rounds, n_outer + 1, rows, sub), jnp.bfloat16),
            pltpu.SemaphoreType.DMA,
            pltpu.SemaphoreType.DMA((2,)),
            pltpu.SemaphoreType.DMA,
            pltpu.SemaphoreType.DMA((rounds, n_outer)),
            pltpu.SemaphoreType.DMA,
            pltpu.SemaphoreType.DMA((rounds, n_outer + 1)),
            pltpu.SemaphoreType.DMA,
        ],
        compiler_params=pltpu.CompilerParams(
            collective_id=0, has_side_effects=True, vmem_limit_bytes=62 * 1024 * 1024
        ),
        cost_estimate=pl.CostEstimate(
            flops=2 * tok_count * depth * total_width,
            bytes_accessed=2 * depth * total_width,
            transcendentals=0,
        ),
        name="reduced_product",
    )(hidden, down_matrix)


def fetch_rows(pool, my_slots, other_slots, half, size):
    per = pool.shape[0]
    low = half * per

    def local(slots):
        return pool[jnp.clip(slots - low, 0, per - 1)]

    rows = local(my_slots)
    got_rows = []
    for shift in range(1, size):
        pairs = [(r, (r - shift) % size) for r in range(size)]
        got_rows.append(lax.ppermute(local(other_slots[shift - 1]), "req", pairs))
    for shift in range(1, size):
        theirs = my_slots // per == (half + shift) % size
        rows = jnp.where(theirs[:, None, None], got_rows[shift - 1], rows)
    return rows


def make_per_device(n_tensor, n_req):
    def per_device(
        hidden,
        down_matrix,
        shrink_factors,
        expand_factors,
        request_adapter,
        request_lengths,
        adapter_rank_table,
        adapter_stored_row,
    ):
        tok_count = hidden.shape[0]
        req_count = request_adapter.shape[1]
        largest_rank = shrink_factors.shape[1]
        local_width = expand_factors.shape[2]
        half = lax.axis_index("req")
        all_ids = lax.all_gather(request_adapter[0], "req", axis=0)
        my_ids = request_adapter[0]
        my_ranks = lookup(adapter_rank_table, my_ids)
        my_slots = lookup(adapter_stored_row, my_ids)
        other_slots = [
            lookup(adapter_stored_row, all_ids[(half - shift) % n_req]) for shift in range(1, n_req)
        ]
        adapter_shrink_rows = fetch_rows(shrink_factors, my_slots, other_slots, half, n_req)
        adapter_expand_rows = fetch_rows(expand_factors, my_slots, other_slots, half, n_req)
        onehot = token_layout(request_lengths, req_count, tok_count)
        flat_a = adapter_shrink_rows.reshape(req_count * largest_rank, adapter_shrink_rows.shape[2])
        shrink_all = lax.dot_general(
            hidden, flat_a, (((1,), (1,)), ((), ())), preferred_element_type=jnp.float32
        )
        shrink_all = shrink_all.reshape(tok_count, req_count, largest_rank)
        live = jnp.arange(largest_rank, dtype=jnp.int32)[None, None, :] < my_ranks[None, :, None]
        keep_mask = onehot[:, :, None] & live
        shrink_result = jnp.sum(jnp.where(keep_mask, shrink_all, 0.0), axis=1)
        token_rank = jnp.sum(jnp.where(onehot, my_ranks[None, :], 0), axis=1)
        token_scale = adapter_scale_factor / token_rank.astype(jnp.float32)
        hidden, shrink_result = lax.optimization_barrier((hidden, shrink_result))
        folded = lax.psum(shrink_result.reshape(tok_count // 2, 2 * largest_rank), "tensor")
        base = reduced_product(hidden, down_matrix, n_tensor)
        scaled_result = (folded.reshape(tok_count, largest_rank) * token_scale[:, None]).astype(
            jnp.bfloat16
        )
        token_spread = jnp.where(
            onehot[:, :, None], scaled_result[:, None, :], jnp.zeros((), jnp.bfloat16)
        )
        token_spread = token_spread.reshape(tok_count, req_count * largest_rank)
        flattened_expand = adapter_expand_rows.reshape(req_count * largest_rank, local_width)
        adapter_piece = jnp.dot(token_spread, flattened_expand, preferred_element_type=jnp.float32)
        return (base + adapter_piece).astype(jnp.bfloat16)

    return per_device


def solution(mesh):
    in_specs = (
        P(("groups", "req"), "tensor"),
        P("tensor", None),
        P("req", None, "tensor"),
        P("req", None, "tensor"),
        P(("groups", "req"), None),
        P(("groups", "req"), None),
        P(),
        P(),
    )
    out_specs = P(("groups", "req"), "tensor")
    per_device = make_per_device(mesh.shape["tensor"], mesh.shape["req"])
    return jax.shard_map(
        per_device, mesh=mesh, in_specs=in_specs, out_specs=out_specs, check_vma=False
    )
```

```python
import functools

import jax
import jax.numpy as jnp
from jax import lax
from jax.experimental import pallas as pl
from jax.experimental.pallas import tpu as pltpu
from jax.sharding import PartitionSpec as P

adapter_scale_factor = 16.0
ROWS = 256
DOT_ROWS = 1024
MESH = pl.DeviceIdType.MESH
ZFIRST = 0


def lookup(values_table, id_list):
    matches = id_list[:, None] == jnp.arange(values_table.shape[0], dtype=jnp.int32)[None, :]
    return jnp.sum(jnp.where(matches, values_table[None, :], 0), axis=1)


def token_layout(request_lengths, req_count, tok_count):
    seg_ends = jnp.cumsum(request_lengths[0])
    positions = jnp.arange(tok_count, dtype=jnp.int32)
    req_of_tok = jnp.sum((positions[:, None] >= seg_ends[None, :]).astype(jnp.int32), axis=1)
    return req_of_tok[:, None] == jnp.arange(req_count, dtype=jnp.int32)[None, :]


def reduce_kernel(
    n_outer,
    rows,
    sub,
    hidden_hbm,
    down_hbm,
    out_hbm,
    hidden,
    tiles,
    y_send,
    y_got,
    own,
    z_got,
    load_sem,
    tile_sems,
    y_send_sem,
    y_got_sems,
    z_send_sem,
    z_got_sems,
    out_sem,
):
    tok_count = hidden.shape[0]
    pieces = tok_count // rows
    rounds = y_send.shape[0]
    chunks = rounds // pieces
    width = chunks * sub
    me = lax.axis_index("tensor")
    z, y = me // 2, me % 2
    last = n_outer - 1

    def device(index):
        return {"tensor": index}

    pair = z * 2 + (1 - y)
    above = (z + 1) * 2 + y
    below = (z - 1) * 2 + y

    def weights(dest_z, dest_y, chunk, slot):
        start = pl.multiple_of((dest_z * 2 + dest_y) * width + chunk * sub, 128)
        return pltpu.make_async_copy(
            down_hbm.at[:, pl.ds(start, sub)], tiles.at[slot], tile_sems.at[slot]
        )

    load = pltpu.make_async_copy(hidden_hbm, hidden, load_sem)
    load.start()
    weights(0, 1 - y, 0, 0).start()

    barrier = pltpu.get_barrier_semaphore()
    pl.semaphore_signal(barrier, inc=1, device_id=device(pair), device_id_type=MESH)

    @pl.when(z < last)
    def _():
        pl.semaphore_signal(barrier, inc=1, device_id=device(above), device_id_type=MESH)

    @pl.when(z > 0)
    def _():
        pl.semaphore_signal(barrier, inc=1, device_id=device(below), device_id_type=MESH)

    pl.semaphore_wait(barrier, 1 + jnp.minimum(z, 1) + jnp.minimum(last - z, 1))

    load.wait()

    def y_copy(rnd, dest):
        return pltpu.make_async_remote_copy(
            src_ref=y_send.at[rnd, dest],
            dst_ref=y_got.at[rnd, dest],
            send_sem=y_send_sem,
            recv_sem=y_got_sems.at[rnd, dest],
            device_id=device(pair),
            device_id_type=MESH,
        )

    def z_copy(rnd, dest, slot, target):
        return pltpu.make_async_remote_copy(
            src_ref=y_got.at[rnd, dest],
            dst_ref=z_got.at[rnd, slot],
            send_sem=z_send_sem,
            recv_sem=z_got_sems.at[rnd, slot],
            device_id=device(target),
            device_id_type=MESH,
        )

    group = min(pieces, DOT_ROWS // rows)

    def product(slot, chunk, dest, store):
        @pl.loop(0, pieces // group)
        def _(part):
            first = pl.multiple_of(part * group * rows, group * rows)
            result = jnp.dot(
                hidden[pl.ds(first, group * rows), :],
                tiles[slot],
                preferred_element_type=jnp.float32,
            )
            for piece in range(group):
                store(
                    chunk * pieces + part * group + piece,
                    dest,
                    result[piece * rows : (piece + 1) * rows],
                )

    total_tiles = chunks * n_outer

    @pl.loop(0, total_tiles)
    def _(index):
        chunk, dest = index // n_outer, index % n_outer
        slot = index % 2

        @pl.when(index + 1 < total_tiles)
        def _():
            weights((index + 1) % n_outer, 1 - y, (index + 1) // n_outer, (index + 1) % 2).start()

        @pl.when(index + 1 == total_tiles)
        def _():
            weights(0, y, 0, total_tiles % 2).start()

        weights(dest, 1 - y, chunk, slot).wait()

        def store_sent(rnd, dest, block):
            y_send[rnd, dest] = block.astype(jnp.bfloat16)

            @pl.when(chunk == 0)
            def _():
                y_copy(rnd, dest).start()

        product(slot, chunk, dest, store_sent)

        @pl.when((chunk > 0) & (dest == last))
        def _():
            @pl.loop(0, pieces * n_outer)
            def _(item):
                y_copy(chunk * pieces + item // n_outer, item % n_outer).start()

    def store_own(rnd, dest, block):
        own[rnd, dest] = block

    def own_tiles(chunk):
        @pl.loop(0, n_outer)
        def _(dest):
            index = chunk * n_outer + dest
            slot = (total_tiles + index) % 2

            @pl.when(index + 1 < total_tiles)
            def _():
                weights(
                    (index + 1) % n_outer, y, (index + 1) // n_outer, (total_tiles + index + 1) % 2
                ).start()

            weights(dest, y, chunk, slot).wait()

            product(slot, chunk, dest, store_own)

    def out_copy(rnd):
        chunk, piece = rnd // pieces, rnd % pieces
        return pltpu.make_async_copy(
            own.at[rnd, z],
            out_hbm.at[
                pl.ds(pl.multiple_of(piece * rows, rows), rows),
                pl.ds(pl.multiple_of(chunk * sub, 128), sub),
            ],
            out_sem,
        )

    @pl.loop(0, rounds + last)
    def _(step):
        @pl.when((step < rounds) & (step % pieces == 0))
        def _():
            own_tiles(step // pieces)

        @pl.loop(0, n_outer)
        def _(dest):
            def pair_sum(rnd):
                y_copy(rnd, dest).wait_recv()
                own[rnd, dest] = own[rnd, dest] + y_got[rnd, dest].astype(jnp.float32)

            def add_line(rnd, slot):
                z_copy(rnd, dest, slot, pair).wait_recv()
                own[rnd, dest] = own[rnd, dest] + z_got[rnd, slot].astype(jnp.float32)

            up_round = step - z

            @pl.when((dest > z) & (up_round >= 0) & (up_round < rounds))
            def _():
                pair_sum(up_round)

                @pl.when(z > 0)
                def _():
                    add_line(up_round, dest)

                y_got[up_round, dest] = own[up_round, dest].astype(jnp.bfloat16)
                z_copy(up_round, dest, dest, above).start()

            down_round = step - (last - z)

            @pl.when((dest < z) & (down_round >= 0) & (down_round < rounds))
            def _():
                pair_sum(down_round)

                @pl.when(z < last)
                def _():
                    add_line(down_round, dest)

                y_got[down_round, dest] = own[down_round, dest].astype(jnp.bfloat16)
                slot = jnp.where(dest == z - 1, n_outer, dest)
                z_copy(down_round, dest, slot, below).start()

            end_round = step - jnp.maximum(z, last - z)

            @pl.when((dest == z) & (end_round >= 0) & (end_round < rounds))
            def _():
                pair_sum(end_round)

                @pl.when(z > 0)
                def _():
                    add_line(end_round, dest)

                @pl.when(z < last)
                def _():
                    add_line(end_round, n_outer)

                out_copy(end_round).start()

    pltpu.make_async_copy(y_send, y_got, y_send_sem).wait()

    if last > 0:
        moved = z_got.at[:, pl.ds(0, last)]
        pltpu.make_async_copy(moved, moved, z_send_sem).wait()

    pltpu.make_async_copy(out_hbm, out_hbm, out_sem).wait()


def reduced_product(hidden, down_matrix, n_tensor):
    tok_count, depth = hidden.shape
    total_width = down_matrix.shape[1]
    width = total_width // n_tensor
    n_outer = n_tensor // 2
    sub = min(256, width)
    rows = min(ROWS, tok_count)
    rounds = (width // sub) * (tok_count // rows)
    return pl.pallas_call(
        functools.partial(reduce_kernel, n_outer, rows, sub),
        out_shape=jax.ShapeDtypeStruct((tok_count, width), jnp.float32),
        in_specs=[pl.BlockSpec(memory_space=pl.ANY)] * 2,
        out_specs=pl.BlockSpec(memory_space=pl.ANY),
        scratch_shapes=[
            pltpu.VMEM((tok_count, depth), jnp.bfloat16),
            pltpu.VMEM((2, depth, sub), jnp.bfloat16),
            pltpu.VMEM((rounds, n_outer, rows, sub), jnp.bfloat16),
            pltpu.VMEM((rounds, n_outer, rows, sub), jnp.bfloat16),
            pltpu.VMEM((rounds, n_outer, rows, sub), jnp.float32),
            pltpu.VMEM((rounds, n_outer + 1, rows, sub), jnp.bfloat16),
            pltpu.SemaphoreType.DMA,
            pltpu.SemaphoreType.DMA((2,)),
            pltpu.SemaphoreType.DMA,
            pltpu.SemaphoreType.DMA((rounds, n_outer)),
            pltpu.SemaphoreType.DMA,
            pltpu.SemaphoreType.DMA((rounds, n_outer + 1)),
            pltpu.SemaphoreType.DMA,
        ],
        compiler_params=pltpu.CompilerParams(
            collective_id=0, has_side_effects=True, vmem_limit_bytes=62 * 1024 * 1024
        ),
        cost_estimate=pl.CostEstimate(
            flops=2 * tok_count * depth * total_width,
            bytes_accessed=2 * depth * total_width,
            transcendentals=0,
        ),
        name="reduced_product",
    )(hidden, down_matrix)


def rows_kernel(slots, pool_a, pool_b, rows_a, rows_b):
    rows_a[...] = pool_a[...]
    rows_b[...] = pool_b[...]


def local_rows(pool_a, pool_b, slots):
    count = slots.shape[0]
    block_a, block_b = (1,) + pool_a.shape[1:], (1,) + pool_b.shape[1:]
    return pl.pallas_call(
        rows_kernel,
        out_shape=[
            jax.ShapeDtypeStruct((count,) + pool_a.shape[1:], pool_a.dtype),
            jax.ShapeDtypeStruct((count,) + pool_b.shape[1:], pool_b.dtype),
        ],
        grid_spec=pltpu.PrefetchScalarGridSpec(
            num_scalar_prefetch=1,
            grid=(count,),
            in_specs=[
                pl.BlockSpec(block_a, lambda step, slots: (slots[step], 0, 0)),
                pl.BlockSpec(block_b, lambda step, slots: (slots[step], 0, 0)),
            ],
            out_specs=[
                pl.BlockSpec(block_a, lambda step, slots: (step, 0, 0)),
                pl.BlockSpec(block_b, lambda step, slots: (step, 0, 0)),
            ],
        ),
        cost_estimate=pl.CostEstimate(
            flops=0,
            bytes_accessed=4 * count * (pool_a[0].size + pool_b[0].size),
            transcendentals=0,
        ),
        name="local_rows",
    )(slots, pool_a, pool_b)


def fetch_rows(pool_a, pool_b, my_slots, other_slots, half, size):
    per = pool_a.shape[0]
    low = half * per

    def local(slots):
        return local_rows(pool_a, pool_b, jnp.clip(slots - low, 0, per - 1))

    got_rows = []
    for shift in range(1, size):
        pairs = [(r, (r - shift) % size) for r in range(size)]
        got_rows.append([lax.ppermute(rows, "req", pairs) for rows in local(other_slots[shift - 1])])
    both = local(my_slots)
    for shift in range(1, size):
        theirs = (my_slots // per == (half + shift) % size)[:, None, None]
        both = [jnp.where(theirs, got, rows) for got, rows in zip(got_rows[shift - 1], both)]
    return both


def make_per_device(n_tensor, n_req):
    def per_device(
        hidden,
        down_matrix,
        shrink_factors,
        expand_factors,
        request_adapter,
        request_lengths,
        adapter_rank_table,
        adapter_stored_row,
    ):
        tok_count = hidden.shape[0]
        req_count = request_adapter.shape[1]
        largest_rank = shrink_factors.shape[1]
        local_width = expand_factors.shape[2]
        half = lax.axis_index("req")
        all_ids = lax.all_gather(request_adapter[0], "req", axis=0)
        my_ids = request_adapter[0]
        my_ranks = lookup(adapter_rank_table, my_ids)
        my_slots = lookup(adapter_stored_row, my_ids)
        other_slots = [
            lookup(adapter_stored_row, all_ids[(half - shift) % n_req]) for shift in range(1, n_req)
        ]
        adapter_shrink_rows, adapter_expand_rows = fetch_rows(
            shrink_factors, expand_factors, my_slots, other_slots, half, n_req
        )
        onehot = token_layout(request_lengths, req_count, tok_count)
        flat_a = adapter_shrink_rows.reshape(req_count * largest_rank, adapter_shrink_rows.shape[2])
        shrink_all = lax.dot_general(
            hidden, flat_a, (((1,), (1,)), ((), ())), preferred_element_type=jnp.float32
        )
        shrink_all = shrink_all.reshape(tok_count, req_count, largest_rank)
        live = jnp.arange(largest_rank, dtype=jnp.int32)[None, None, :] < my_ranks[None, :, None]
        keep_mask = onehot[:, :, None] & live
        shrink_result = jnp.sum(jnp.where(keep_mask, shrink_all, 0.0), axis=1)
        token_rank = jnp.sum(jnp.where(onehot, my_ranks[None, :], 0), axis=1)
        token_scale = adapter_scale_factor / token_rank.astype(jnp.float32)
        hidden, shrink_result = lax.optimization_barrier((hidden, shrink_result))
        folded = lax.psum(shrink_result.reshape(tok_count // 2, 2 * largest_rank), "tensor")
        base = reduced_product(hidden, down_matrix, n_tensor)
        scaled_result = (folded.reshape(tok_count, largest_rank) * token_scale[:, None]).astype(
            jnp.bfloat16
        )
        token_spread = jnp.where(
            onehot[:, :, None], scaled_result[:, None, :], jnp.zeros((), jnp.bfloat16)
        )
        token_spread = token_spread.reshape(tok_count, req_count * largest_rank)
        flattened_expand = adapter_expand_rows.reshape(req_count * largest_rank, local_width)
        adapter_piece = jnp.dot(token_spread, flattened_expand, preferred_element_type=jnp.float32)
        return (base + adapter_piece).astype(jnp.bfloat16)

    return per_device


def solution(mesh):
    in_specs = (
        P(("groups", "req"), "tensor"),
        P("tensor", None),
        P("req", None, "tensor"),
        P("req", None, "tensor"),
        P(("groups", "req"), None),
        P(("groups", "req"), None),
        P(),
        P(),
    )
    out_specs = P(("groups", "req"), "tensor")
    per_device = make_per_device(mesh.shape["tensor"], mesh.shape["req"])
    return jax.shard_map(
        per_device, mesh=mesh, in_specs=in_specs, out_specs=out_specs, check_vma=False
    )
```

```python
import functools

import jax
import jax.numpy as jnp
from jax import lax
from jax.experimental import pallas as pl
from jax.experimental.pallas import tpu as pltpu
from jax.sharding import PartitionSpec as P

adapter_scale_factor = 16.0
ROWS = 256
DOT_ROWS = 1024
MESH = pl.DeviceIdType.MESH
ZFIRST = 0


def lookup(values_table, id_list):
    matches = id_list[:, None] == jnp.arange(values_table.shape[0], dtype=jnp.int32)[None, :]
    return jnp.sum(jnp.where(matches, values_table[None, :], 0), axis=1)


def token_layout(request_lengths, req_count, tok_count):
    seg_ends = jnp.cumsum(request_lengths[0])
    positions = jnp.arange(tok_count, dtype=jnp.int32)
    req_of_tok = jnp.sum((positions[:, None] >= seg_ends[None, :]).astype(jnp.int32), axis=1)
    return req_of_tok[:, None] == jnp.arange(req_count, dtype=jnp.int32)[None, :]


def reduce_kernel(
    n_outer,
    rows,
    sub,
    hidden_hbm,
    down_hbm,
    out_hbm,
    hidden,
    tiles,
    y_send,
    y_got,
    own,
    z_got,
    load_sem,
    tile_sems,
    y_send_sem,
    y_got_sems,
    z_send_sem,
    z_got_sems,
    out_sem,
):
    tok_count = hidden.shape[0]
    pieces = tok_count // rows
    rounds = y_send.shape[0]
    chunks = rounds // pieces
    width = chunks * sub
    me = lax.axis_index("tensor")
    z, y = me // 2, me % 2
    last = n_outer - 1

    def device(index):
        return {"tensor": index}

    pair = z * 2 + (1 - y)
    above = (z + 1) * 2 + y
    below = (z - 1) * 2 + y

    def weights(dest_z, dest_y, chunk, slot):
        start = pl.multiple_of((dest_z * 2 + dest_y) * width + chunk * sub, 128)
        return pltpu.make_async_copy(
            down_hbm.at[:, pl.ds(start, sub)], tiles.at[slot], tile_sems.at[slot]
        )

    load = pltpu.make_async_copy(hidden_hbm, hidden, load_sem)
    load.start()
    weights(0, 1 - y, 0, 0).start()

    barrier = pltpu.get_barrier_semaphore()
    pl.semaphore_signal(barrier, inc=1, device_id=device(pair), device_id_type=MESH)

    @pl.when(z < last)
    def _():
        pl.semaphore_signal(barrier, inc=1, device_id=device(above), device_id_type=MESH)

    @pl.when(z > 0)
    def _():
        pl.semaphore_signal(barrier, inc=1, device_id=device(below), device_id_type=MESH)

    pl.semaphore_wait(barrier, 1 + jnp.minimum(z, 1) + jnp.minimum(last - z, 1))

    load.wait()

    def y_copy(rnd, dest):
        return pltpu.make_async_remote_copy(
            src_ref=y_send.at[rnd, dest],
            dst_ref=y_got.at[rnd, dest],
            send_sem=y_send_sem,
            recv_sem=y_got_sems.at[rnd, dest],
            device_id=device(pair),
            device_id_type=MESH,
        )

    def z_copy(rnd, dest, slot, target):
        return pltpu.make_async_remote_copy(
            src_ref=y_got.at[rnd, dest],
            dst_ref=z_got.at[rnd, slot],
            send_sem=z_send_sem,
            recv_sem=z_got_sems.at[rnd, slot],
            device_id=device(target),
            device_id_type=MESH,
        )

    group = min(pieces, DOT_ROWS // rows)

    def product(slot, chunk, dest, store):
        @pl.loop(0, pieces // group)
        def _(part):
            first = pl.multiple_of(part * group * rows, group * rows)
            result = jnp.dot(
                hidden[pl.ds(first, group * rows), :],
                tiles[slot],
                preferred_element_type=jnp.float32,
            )
            for piece in range(group):
                store(
                    chunk * pieces + part * group + piece,
                    dest,
                    result[piece * rows : (piece + 1) * rows],
                )

    total_tiles = chunks * n_outer

    @pl.loop(0, total_tiles)
    def _(index):
        chunk, dest = index // n_outer, index % n_outer
        slot = index % 2

        @pl.when(index + 1 < total_tiles)
        def _():
            weights((index + 1) % n_outer, 1 - y, (index + 1) // n_outer, (index + 1) % 2).start()

        @pl.when(index + 1 == total_tiles)
        def _():
            weights(0, y, 0, total_tiles % 2).start()

        weights(dest, 1 - y, chunk, slot).wait()

        def store_sent(rnd, dest, block):
            y_send[rnd, dest] = block.astype(jnp.bfloat16)

            @pl.when(chunk == 0)
            def _():
                y_copy(rnd, dest).start()

        product(slot, chunk, dest, store_sent)

        @pl.when((chunk > 0) & (dest == last))
        def _():
            @pl.loop(0, pieces * n_outer)
            def _(item):
                y_copy(chunk * pieces + item // n_outer, item % n_outer).start()

    def store_own(rnd, dest, block):
        own[rnd, dest] = block

    def own_tiles(chunk):
        @pl.loop(0, n_outer)
        def _(dest):
            index = chunk * n_outer + dest
            slot = (total_tiles + index) % 2

            @pl.when(index + 1 < total_tiles)
            def _():
                weights(
                    (index + 1) % n_outer, y, (index + 1) // n_outer, (total_tiles + index + 1) % 2
                ).start()

            weights(dest, y, chunk, slot).wait()

            product(slot, chunk, dest, store_own)

    def out_copy(rnd):
        chunk, piece = rnd // pieces, rnd % pieces
        return pltpu.make_async_copy(
            own.at[rnd, z],
            out_hbm.at[
                pl.ds(pl.multiple_of(piece * rows, rows), rows),
                pl.ds(pl.multiple_of(chunk * sub, 128), sub),
            ],
            out_sem,
        )

    @pl.loop(0, rounds + last)
    def _(step):
        @pl.when((step < rounds) & (step % pieces == 0))
        def _():
            own_tiles(step // pieces)

        @pl.loop(0, n_outer)
        def _(dest):
            def pair_sum(rnd):
                return own[rnd, dest] + y_got[rnd, dest].astype(jnp.float32)

            def pass_on(rnd, first):
                y_copy(rnd, dest).wait_recv()

                @pl.when(first)
                def _():
                    y_got[rnd, dest] = pair_sum(rnd).astype(jnp.bfloat16)

                @pl.when(jnp.logical_not(first))
                def _():
                    z_copy(rnd, dest, dest, pair).wait_recv()
                    total = pair_sum(rnd) + z_got[rnd, dest].astype(jnp.float32)
                    y_got[rnd, dest] = total.astype(jnp.bfloat16)

            def add_line(rnd, slot):
                z_copy(rnd, dest, slot, pair).wait_recv()
                own[rnd, dest] = own[rnd, dest] + z_got[rnd, slot].astype(jnp.float32)

            up_round = step - z

            @pl.when((dest > z) & (up_round >= 0) & (up_round < rounds))
            def _():
                pass_on(up_round, z == 0)
                z_copy(up_round, dest, dest, above).start()

            down_round = step - (last - z)

            @pl.when((dest < z) & (down_round >= 0) & (down_round < rounds))
            def _():
                pass_on(down_round, z == last)
                slot = jnp.where(dest == z - 1, n_outer, dest)
                z_copy(down_round, dest, slot, below).start()

            end_round = step - jnp.maximum(z, last - z)

            @pl.when((dest == z) & (end_round >= 0) & (end_round < rounds))
            def _():
                y_copy(end_round, dest).wait_recv()
                own[end_round, dest] = pair_sum(end_round)

                @pl.when(z > 0)
                def _():
                    add_line(end_round, dest)

                @pl.when(z < last)
                def _():
                    add_line(end_round, n_outer)

                out_copy(end_round).start()

    pltpu.make_async_copy(y_send, y_got, y_send_sem).wait()

    if last > 0:
        moved = z_got.at[:, pl.ds(0, last)]
        pltpu.make_async_copy(moved, moved, z_send_sem).wait()

    pltpu.make_async_copy(out_hbm, out_hbm, out_sem).wait()


def reduced_product(hidden, down_matrix, n_tensor):
    tok_count, depth = hidden.shape
    total_width = down_matrix.shape[1]
    width = total_width // n_tensor
    n_outer = n_tensor // 2
    sub = min(256, width)
    rows = min(ROWS, tok_count)
    rounds = (width // sub) * (tok_count // rows)
    return pl.pallas_call(
        functools.partial(reduce_kernel, n_outer, rows, sub),
        out_shape=jax.ShapeDtypeStruct((tok_count, width), jnp.float32),
        in_specs=[pl.BlockSpec(memory_space=pl.ANY)] * 2,
        out_specs=pl.BlockSpec(memory_space=pl.ANY),
        scratch_shapes=[
            pltpu.VMEM((tok_count, depth), jnp.bfloat16),
            pltpu.VMEM((2, depth, sub), jnp.bfloat16),
            pltpu.VMEM((rounds, n_outer, rows, sub), jnp.bfloat16),
            pltpu.VMEM((rounds, n_outer, rows, sub), jnp.bfloat16),
            pltpu.VMEM((rounds, n_outer, rows, sub), jnp.float32),
            pltpu.VMEM((rounds, n_outer + 1, rows, sub), jnp.bfloat16),
            pltpu.SemaphoreType.DMA,
            pltpu.SemaphoreType.DMA((2,)),
            pltpu.SemaphoreType.DMA,
            pltpu.SemaphoreType.DMA((rounds, n_outer)),
            pltpu.SemaphoreType.DMA,
            pltpu.SemaphoreType.DMA((rounds, n_outer + 1)),
            pltpu.SemaphoreType.DMA,
        ],
        compiler_params=pltpu.CompilerParams(
            collective_id=0, has_side_effects=True, vmem_limit_bytes=62 * 1024 * 1024
        ),
        cost_estimate=pl.CostEstimate(
            flops=2 * tok_count * depth * total_width,
            bytes_accessed=2 * depth * total_width,
            transcendentals=0,
        ),
        name="reduced_product",
    )(hidden, down_matrix)


def rows_kernel(slots, pool_a, pool_b, rows_a, rows_b):
    rows_a[...] = pool_a[...]
    rows_b[...] = pool_b[...]


def local_rows(pool_a, pool_b, slots):
    count = slots.shape[0]
    block_a, block_b = (1,) + pool_a.shape[1:], (1,) + pool_b.shape[1:]
    return pl.pallas_call(
        rows_kernel,
        out_shape=[
            jax.ShapeDtypeStruct((count,) + pool_a.shape[1:], pool_a.dtype),
            jax.ShapeDtypeStruct((count,) + pool_b.shape[1:], pool_b.dtype),
        ],
        grid_spec=pltpu.PrefetchScalarGridSpec(
            num_scalar_prefetch=1,
            grid=(count,),
            in_specs=[
                pl.BlockSpec(block_a, lambda step, slots: (slots[step], 0, 0)),
                pl.BlockSpec(block_b, lambda step, slots: (slots[step], 0, 0)),
            ],
            out_specs=[
                pl.BlockSpec(block_a, lambda step, slots: (step, 0, 0)),
                pl.BlockSpec(block_b, lambda step, slots: (step, 0, 0)),
            ],
        ),
        cost_estimate=pl.CostEstimate(
            flops=0,
            bytes_accessed=4 * count * (pool_a[0].size + pool_b[0].size),
            transcendentals=0,
        ),
        name="local_rows",
    )(slots, pool_a, pool_b)


def fetch_rows(pool_a, pool_b, my_slots, other_slots, half, size):
    per = pool_a.shape[0]
    low = half * per

    def local(slots):
        return local_rows(pool_a, pool_b, jnp.clip(slots - low, 0, per - 1))

    got_rows = []
    for shift in range(1, size):
        pairs = [(r, (r - shift) % size) for r in range(size)]
        got_rows.append([lax.ppermute(rows, "req", pairs) for rows in local(other_slots[shift - 1])])
    both = local(my_slots)
    for shift in range(1, size):
        theirs = (my_slots // per == (half + shift) % size)[:, None, None]
        both = [jnp.where(theirs, got, rows) for got, rows in zip(got_rows[shift - 1], both)]
    return both


def make_per_device(n_tensor, n_req):
    def per_device(
        hidden,
        down_matrix,
        shrink_factors,
        expand_factors,
        request_adapter,
        request_lengths,
        adapter_rank_table,
        adapter_stored_row,
    ):
        tok_count = hidden.shape[0]
        req_count = request_adapter.shape[1]
        largest_rank = shrink_factors.shape[1]
        local_width = expand_factors.shape[2]
        half = lax.axis_index("req")
        all_ids = lax.all_gather(request_adapter[0], "req", axis=0)
        my_ids = request_adapter[0]
        my_ranks = lookup(adapter_rank_table, my_ids)
        my_slots = lookup(adapter_stored_row, my_ids)
        other_slots = [
            lookup(adapter_stored_row, all_ids[(half - shift) % n_req]) for shift in range(1, n_req)
        ]
        adapter_shrink_rows, adapter_expand_rows = fetch_rows(
            shrink_factors, expand_factors, my_slots, other_slots, half, n_req
        )
        onehot = token_layout(request_lengths, req_count, tok_count)
        flat_a = adapter_shrink_rows.reshape(req_count * largest_rank, adapter_shrink_rows.shape[2])
        shrink_all = lax.dot_general(
            hidden, flat_a, (((1,), (1,)), ((), ())), preferred_element_type=jnp.float32
        )
        shrink_all = shrink_all.reshape(tok_count, req_count, largest_rank)
        live = jnp.arange(largest_rank, dtype=jnp.int32)[None, None, :] < my_ranks[None, :, None]
        keep_mask = onehot[:, :, None] & live
        shrink_result = jnp.sum(jnp.where(keep_mask, shrink_all, 0.0), axis=1)
        token_rank = jnp.sum(jnp.where(onehot, my_ranks[None, :], 0), axis=1)
        token_scale = adapter_scale_factor / token_rank.astype(jnp.float32)
        hidden, shrink_result = lax.optimization_barrier((hidden, shrink_result))
        folded = lax.psum(shrink_result.reshape(tok_count // 2, 2 * largest_rank), "tensor")
        base = reduced_product(hidden, down_matrix, n_tensor)
        scaled_result = (folded.reshape(tok_count, largest_rank) * token_scale[:, None]).astype(
            jnp.bfloat16
        )
        token_spread = jnp.where(
            onehot[:, :, None], scaled_result[:, None, :], jnp.zeros((), jnp.bfloat16)
        )
        token_spread = token_spread.reshape(tok_count, req_count * largest_rank)
        flattened_expand = adapter_expand_rows.reshape(req_count * largest_rank, local_width)
        adapter_piece = jnp.dot(token_spread, flattened_expand, preferred_element_type=jnp.float32)
        return (base + adapter_piece).astype(jnp.bfloat16)

    return per_device


def solution(mesh):
    in_specs = (
        P(("groups", "req"), "tensor"),
        P("tensor", None),
        P("req", None, "tensor"),
        P("req", None, "tensor"),
        P(("groups", "req"), None),
        P(("groups", "req"), None),
        P(),
        P(),
    )
    out_specs = P(("groups", "req"), "tensor")
    per_device = make_per_device(mesh.shape["tensor"], mesh.shape["req"])
    return jax.shard_map(
        per_device, mesh=mesh, in_specs=in_specs, out_specs=out_specs, check_vma=False
    )
```
